32 devices in a mesh: groups: 2 (over y), gx: 4 (over z), gy: 2 (over x), sa: 2 (over core).
Axes of the slice: x: 2, y: 2, z: 4, core: 2. Of those that a mesh axis runs over, the one named last changes fastest.
Arguments:
- source_now: float32 [4, 128, 48, 128], P(('groups', 'sa'), 'gx', 'gy'), parts along dimension 0, may hold values from -6 to 6
- source_later: float32 [4, 128, 48, 128], P(('groups', 'sa'), 'gx', 'gy'), parts along dimension 0, may hold values from -6 to 6
- receiver_now: float32 [4, 128, 48, 128], P(('groups', 'sa'), 'gx', 'gy'), parts along dimension 0, may hold values from -6 to 6
- receiver_later: float32 [4, 128, 48, 128], P(('groups', 'sa'), 'gx', 'gy'), parts along dimension 0, may hold values from -6 to 6
- courant: float32 [128, 48, 128], P('gx', 'gy'), may hold values from 0.05 to 0.19
- wavelet: float32 [4, 12], P(('groups', 'sa')), parts along dimension 0, may hold values from -8 to 8
- traces: float32 [4, 12, 64], P(('groups', 'sa')), parts along dimension 0, may hold values from -6 to 6
- source_inline: int32 [4], P(('groups', 'sa')), parts along dimension 0, may hold values from 0 to 127
- source_crossline: int32 [4], P(('groups', 'sa')), parts along dimension 0, may hold values from 0 to 47
- receiver_inline: int32 [4, 64], P(('groups', 'sa')), parts along dimension 0, may hold values from 0 to 127
- receiver_crossline: int32 [4, 64], P(('groups', 'sa')), parts along dimension 0, may hold values from 0 to 47
Outputs:
- source_first: float32 [4, 128, 48, 128], P(('groups', 'sa'), 'gx', 'gy'), parts along dimension 0
- source_second: float32 [4, 128, 48, 128], P(('groups', 'sa'), 'gx', 'gy'), parts along dimension 0
- receiver_first: float32 [4, 128, 48, 128], P(('groups', 'sa'), 'gx', 'gy'), parts along dimension 0
- receiver_second: float32 [4, 128, 48, 128], P(('groups', 'sa'), 'gx', 'gy'), parts along dimension 0
- image_stack: float32 [256, 48, 128], P(('groups', 'gx', 'sa'), 'gy'), parts along dimension 0
The draws below stay inside these ranges and needn't reach their ends.
There are 2 independent parts, one for each index of `groups`. The reference program is written for one: setup_inputs(seed, part) draws one part's arguments, and reference() takes and returns one part's arrays. A program takes and returns all parts, laid end to end along the dimension named above; an argument that names none is the same for every part. Nothing has to cross between parts.
All inputs are finite; a program needn't handle non-finite values.
Results may differ from the reference program's by a relative error of at most 0.0003.
Values sent between devices are 32-bit elements; how exact they have to be, the bound alone decides.
A program may use at most 128 MiB of HBM per device.

```python
import jax
import jax.numpy as jnp

SRC_DEPTH = 3
REC_DEPTH = 2
STEPS = 12
NX = 128
NY = 48
NZ = 128
SHOTS = 2
NREC = 64


def with_ends(drawn, key, low, high):
    extent = drawn.shape
    index_at = [jax.random.randint(jax.random.fold_in(key, axis), (), 0, extent[axis]) for axis in range(len(extent))]
    drawn = drawn.at[tuple(index_at)].set(low)
    longest = extent.index(max(extent))
    index_at[longest] = (index_at[longest] + 1) % extent[longest]
    return drawn.at[tuple(index_at)].set(high)


def block_levels(stream_key, extent, split, least, high):
    factor_of, own = 1.0, jax.random.fold_in(stream_key, 6)
    for position, blocks in split:
        draws = jnp.exp(jax.random.uniform(jax.random.fold_in(own, position), (blocks,), jnp.float32, least / len(split), high / len(split)))
        factor_of = factor_of * jnp.repeat(draws, extent[position] // blocks).reshape([-1 if axis == position else 1 for axis in range(len(extent))])
    return factor_of


def noise(own_key, dims, spread, bound, pieces=(), held_as=jnp.bfloat16):
    result = jax.random.normal(own_key, dims, jnp.float32) * spread
    if len(pieces) > 0:
        result = block_levels(own_key, dims, pieces, -0.22, 0.18) * result
    return jnp.clip(result, min=-bound, max=bound).astype(held_as)


def setup_inputs(seed: int = 0, part: int = 0) -> dict:
    key_list = jax.random.split(jax.random.key(seed), 12)
    part_keys = jax.random.split(jax.random.fold_in(key_list[11], part), 12)
    return {
        "source_now": noise(part_keys[0], (SHOTS, NX, NY, NZ), 1.0, 6.0, ((0, 2), (1, 4), (2, 2)), jnp.float32),
        "source_later": noise(part_keys[1], (SHOTS, NX, NY, NZ), 1.0, 6.0, ((0, 2), (1, 4), (2, 2)), jnp.float32),
        "receiver_now": noise(part_keys[2], (SHOTS, NX, NY, NZ), 1.0, 6.0, ((0, 2), (1, 4), (2, 2)), jnp.float32),
        "receiver_later": noise(part_keys[3], (SHOTS, NX, NY, NZ), 1.0, 6.0, ((0, 2), (1, 4), (2, 2)), jnp.float32),
        "courant": jnp.clip(0.05 + 0.14 * jax.random.uniform(key_list[4], (NX, NY, NZ), jnp.float32) ** block_levels(key_list[4], (NX, NY, NZ), ((0, 4), (1, 2)), -0.2, 0.2), 0.05, 0.19),
        "wavelet": noise(part_keys[5], (SHOTS, STEPS), 2.0, 8.0, ((0, 2),), jnp.float32),
        "traces": noise(part_keys[6], (SHOTS, STEPS, NREC), 1.0, 6.0, ((0, 2),), jnp.float32),
        "source_inline": jax.random.randint(part_keys[7], (SHOTS,), 0, NX).astype(jnp.int32),
        "source_crossline": jax.random.randint(part_keys[8], (SHOTS,), 0, NY).astype(jnp.int32),
        "receiver_inline": with_ends(jax.random.randint(part_keys[9], (SHOTS, NREC), 0, NX), jax.random.fold_in(part_keys[9], 1), 0, NX - 1).astype(jnp.int32),
        "receiver_crossline": with_ends(jax.random.randint(part_keys[10], (SHOTS, NREC), 0, NY), jax.random.fold_in(part_keys[10], 1), 0, NY - 1).astype(jnp.int32),
    }


COEFFS = (-205.0 / 72.0, 8.0 / 5.0, -1.0 / 5.0, 8.0 / 315.0, -1.0 / 560.0)


def laplace(padded):
    inline_span = padded.shape[0] - 8
    cross_span = padded.shape[1] - 8
    center = padded[4:4 + inline_span, 4:4 + cross_span]
    depth_span = center.shape[2]
    depth_padded = jnp.pad(center, ((0, 0), (0, 0), (4, 4)))
    summed = (3.0 * COEFFS[0]) * center
    for distance in range(1, 5):
        neighbours = padded[4 + distance:4 + distance + inline_span, 4:4 + cross_span] + padded[4 - distance:4 - distance + inline_span, 4:4 + cross_span]
        neighbours = neighbours + padded[4:4 + inline_span, 4 + distance:4 + distance + cross_span] + padded[4:4 + inline_span, 4 - distance:4 - distance + cross_span]
        neighbours = neighbours + depth_padded[:, :, 4 + distance:4 + distance + depth_span] + depth_padded[:, :, 4 - distance:4 - distance + depth_span]
        summed = summed + COEFFS[distance] * neighbours
    return summed


def reference(source_now, source_later, receiver_now, receiver_later, courant, wavelet, traces, source_inline, source_crossline, receiver_inline, receiver_crossline):
    depth_axis = jnp.arange(NZ)
    source_layer = (depth_axis == SRC_DEPTH).astype(jnp.float32)
    receiver_layer = (depth_axis == REC_DEPTH).astype(jnp.float32)
    widths = ((4, 4), (4, 4), (0, 0))
    firsts_source, seconds_source, firsts_receiver, seconds_receiver = [], [], [], []
    image_total = jnp.zeros((NX, NY, NZ), jnp.float32)
    for shot_index in range(SHOTS):
        source_field = source_now[shot_index]
        source_prior = source_later[shot_index]
        receiver_field = receiver_now[shot_index]
        receiver_prior = receiver_later[shot_index]
        source_spot = jnp.zeros((NX, NY), jnp.float32).at[source_inline[shot_index], source_crossline[shot_index]].set(1.0)
        record_planes = jnp.zeros((STEPS, NX, NY), jnp.float32).at[:, receiver_inline[shot_index], receiver_crossline[shot_index]].add(traces[shot_index])
        correlation = jnp.zeros((NX, NY, NZ), jnp.float32)
        for moment in range(STEPS):
            source_curve = laplace(jnp.pad(source_field, widths))
            source_new = 2.0 * source_field - source_prior + courant * (source_curve + (wavelet[shot_index, moment] * source_spot)[:, :, None] * source_layer)
            receiver_curve = laplace(jnp.pad(receiver_field, widths))
            receiver_new = 2.0 * receiver_field - receiver_prior + courant * (receiver_curve + record_planes[moment][:, :, None] * receiver_layer)
            correlation = correlation + source_new * receiver_new
            source_prior, source_field = source_field, source_new
            receiver_prior, receiver_field = receiver_field, receiver_new
        firsts_source.append(source_field)
        seconds_source.append(source_prior)
        firsts_receiver.append(receiver_field)
        seconds_receiver.append(receiver_prior)
        image_total = image_total + correlation
    image_stack = image_total / STEPS
    return (jnp.stack(firsts_source), jnp.stack(seconds_source), jnp.stack(firsts_receiver), jnp.stack(seconds_receiver), image_stack)
```

```python
import functools

import jax
import jax.numpy as jnp
from jax import lax
from jax.experimental import pallas as pl
from jax.experimental.pallas import tpu as pltpu
from jax.sharding import PartitionSpec as P

SRC_DEPTH = 3
REC_DEPTH = 2
STEPS = 12
REACH = 4
SIDE = 8
PLANES = 4

COEFFS = (-205.0 / 72.0, 8.0 / 5.0, -1.0 / 5.0, 8.0 / 315.0, -1.0 / 560.0)
MESH = pl.DeviceIdType.MESH
BF16 = jnp.bfloat16
F32 = jnp.float32


def halves(values):
    high = values.astype(BF16)
    low = (values - high.astype(F32)).astype(BF16)
    return high, low


def kernel(
    s_now, s_later, r_now, r_later, speed_in,
    wave, traces, s_in, s_cr, r_in, r_cr,
    s_first, s_second, r_first, r_second, image,
    s0, s1, r0, r1, speed, corr, other, mine, q_s, q_r, w_main, w_side,
    x_out, x_in, load_sem, send_sem, recv_sem, sum_sem, store_sem,
):
    ni, nc, nz = speed.shape
    cells = ni * nc
    half = ni // 2
    gx, gy, sa = lax.axis_index("gx"), lax.axis_index("gy"), lax.axis_index("sa")
    last_x, last_y = lax.axis_size("gx") - 1, lax.axis_size("gy") - 1
    below, above = gx > 0, gx < last_x
    left, right = gy > 0, gy < last_y
    fields = ((s0, s1), (r0, r1))
    rows = pl.ds(SIDE, nc)
    inner = (pl.ds(REACH, ni), rows)

    loads = [
        pltpu.make_async_copy(src, dst, load_sem.at[n])
        for n, (src, dst) in enumerate(
            (
                (s_now, s0.at[inner]),
                (r_now, r0.at[inner]),
                (s_later, s1.at[inner]),
                (r_later, r1.at[inner]),
                (speed_in, speed),
            )
        )
    ]
    for load in loads:
        load.start()

    ways = (
        ({"gx": gx - 1}, below, above),
        ({"gx": gx + 1}, above, below),
        ({"gy": gy - 1}, left, right),
        ({"gy": gy + 1}, right, left),
    )
    barrier = pltpu.get_barrier_semaphore()
    for target, sends, _ in ways:
        @pl.when(sends)
        def _():
            pl.semaphore_signal(barrier, inc=1, device_id=target, device_id_type=MESH)
    pl.semaphore_signal(barrier, inc=1, device_id={"sa": 1 - sa}, device_id_type=MESH)

    def exchange(field, slot, way):
        buf = fields[field][slot]
        if way == 0:
            src, dst = buf.at[pl.ds(REACH, REACH), rows], buf.at[pl.ds(REACH + ni, REACH), rows]
        elif way == 1:
            src, dst = buf.at[pl.ds(ni, REACH), rows], buf.at[pl.ds(0, REACH), rows]
        else:
            src, dst = x_out.at[field, slot, way - 2], x_in.at[field, slot, way - 2]
        return pltpu.make_async_remote_copy(
            src_ref=src, dst_ref=dst,
            send_sem=send_sem.at[field, slot, way], recv_sem=recv_sem.at[field, slot, way],
            device_id=ways[way][0], device_id_type=MESH,
        )

    def send(field, slot):
        buf = fields[field][slot]
        for way in (2, 3, 0, 1):
            @pl.when(ways[way][1])
            def _():
                if way == 2:
                    x_out[field, slot, 0] = buf[REACH:REACH + ni, SIDE:SIDE + REACH, :]
                if way == 3:
                    x_out[field, slot, 1] = buf[REACH:REACH + ni, SIDE + nc - REACH:SIDE + nc, :]
                exchange(field, slot, way).start()

    def sent(field, slot):
        for way in range(4):
            @pl.when(ways[way][1])
            def _():
                exchange(field, slot, way).wait_send()

    def receive(field, slot):
        buf = fields[field][slot]
        for way in (2, 3, 0, 1):
            @pl.when(ways[way][2])
            def _():
                exchange(field, slot, way).wait_recv()
                if way == 2:
                    buf[REACH:REACH + ni, SIDE + nc:SIDE + nc + REACH, :] = x_in[field, slot, 0]
                if way == 3:
                    buf[REACH:REACH + ni, SIDE - REACH:SIDE, :] = x_in[field, slot, 1]

    for pair in fields:
        for buf in pair:
            @pl.when(jnp.logical_not(below))
            def _():
                buf[0:REACH, SIDE:SIDE + nc, :] = jnp.zeros((REACH, nc, nz), F32)
            @pl.when(jnp.logical_not(above))
            def _():
                buf[REACH + ni:, SIDE:SIDE + nc, :] = jnp.zeros((REACH, nc, nz), F32)
            @pl.when(jnp.logical_not(left))
            def _():
                buf[REACH:REACH + ni, SIDE - REACH:SIDE, :] = jnp.zeros((ni, REACH, nz), F32)
            @pl.when(jnp.logical_not(right))
            def _():
                buf[REACH:REACH + ni, SIDE + nc:SIDE + nc + REACH, :] = jnp.zeros((ni, REACH, nz), F32)

    peers = 1
    for _, sends, _ in ways:
        peers = peers + sends.astype(jnp.int32)
    pl.semaphore_wait(barrier, peers)
    loads[0].wait()
    send(0, 0)
    loads[1].wait()
    send(1, 0)

    line = lax.broadcasted_iota(jnp.int32, (nz, nz), 0)
    lane = lax.broadcasted_iota(jnp.int32, (nz, nz), 1)
    apart = jnp.abs(line - lane)
    band = jnp.where(apart == 0, 3.0 * COEFFS[0], 0.0)
    for distance in range(1, 5):
        band = jnp.where(apart == distance, COEFFS[distance], band)
    band_high, band_low = halves(band.astype(F32))
    w_main[0:nz, :] = band_high
    w_main[nz:, :] = band_high
    for field in range(2):
        w_side[field, 0:nz, :] = band_low

    pick = (lax.broadcasted_iota(jnp.int32, (nz, STEPS), 0) % 32
            == lax.broadcasted_iota(jnp.int32, (nz, STEPS), 1)).astype(F32)
    dot = functools.partial(lax.dot_general, precision=lax.Precision.HIGHEST, preferred_element_type=F32)
    by_lane = dot(pick, traces[0], (((1,), (0,)), ((), ())))
    wave_lane = dot(jnp.broadcast_to(wave[...], (8, STEPS)), pick, (((1,), (1,)), ((), ())))[0:1]

    def local(inline, cross):
        a, b = inline - gx * ni, cross - gy * nc
        inside = (a >= 0) & (a < ni) & (b >= 0) & (b < nc)
        return jnp.where(inside, a * nc + b, -1)

    where_r = local(r_in[...], r_cr[...])
    where_s = local(s_in[0], s_cr[0])
    part = PLANES * nc

    def terms(total):
        group = lax.broadcasted_iota(jnp.int32, (part, nz), 1) // 32
        first = total.astype(BF16).astype(F32)
        rest = total - first
        second = rest.astype(BF16).astype(F32)
        third = rest - second
        return jnp.where(group == 0, first, jnp.where(group == 1, second, jnp.where(group == 2, third, 0.0))).astype(BF16)

    @pl.loop(0, cells // part)
    def _(n):
        start = pl.multiple_of(n * part, part)
        index = lax.broadcasted_iota(jnp.int32, (part, 1), 0) + start
        hot = (index == where_r).astype(F32)
        q_r[pl.ds(start, part), :] = terms(dot(hot, by_lane, (((1,), (1,)), ((), ()))))
        q_s[pl.ds(start, part), :] = terms(jnp.where(index == where_s, wave_lane, 0.0))

    corr[...] = jnp.zeros_like(corr)
    for load in loads[2:]:
        load.wait()

    mul = functools.partial(jnp.dot, preferred_element_type=F32)

    def advance(field, slot, moment):
        cur, new = fields[field][slot], fields[field][1 - slot]
        depth = (SRC_DEPTH, REC_DEPTH)[field]
        q = (q_s, q_r)[field]
        spot = (line < 96) & (line % 32 == moment) & (lane == depth)
        w_side[field, nz:, :] = spot.astype(F32).astype(BF16)
        main, side = w_main[...], w_side[field]
        for low in range(0, ni, PLANES):
            at = low + REACH
            here = slice(at, at + PLANES)
            centre = cur[here, SIDE:SIDE + nc, :]
            high_part, low_part = halves(centre.reshape(part, nz))
            total = mul(jnp.concatenate([high_part, low_part], axis=1), main)
            total = total + mul(
                jnp.concatenate([high_part, q[low * nc:low * nc + part, :]], axis=1), side
            )
            total = total.reshape(PLANES, nc, nz)
            for k in range(1, 5):
                around = (
                    cur[at + k:at + k + PLANES, SIDE:SIDE + nc, :]
                    + cur[at - k:at - k + PLANES, SIDE:SIDE + nc, :]
                ) + (cur[here, SIDE + k:SIDE + k + nc, :] + cur[here, SIDE - k:SIDE - k + nc, :])
                total = total + COEFFS[k] * around
            fresh = 2.0 * centre - new[here, SIDE:SIDE + nc, :] + speed[low:low + PLANES] * total
            new[here, SIDE:SIDE + nc, :] = fresh
            if field == 1:
                corr[low:low + PLANES] += fresh * s_at(slot)[here, SIDE:SIDE + nc, :]

    def s_at(slot):
        return fields[0][1 - slot]

    @pl.loop(0, STEPS // 2)
    def _(pair):
        for slot in range(2):
            for field in range(2):
                receive(field, slot)
                if slot == 0:
                    @pl.when(pair > 0)
                    def _():
                        sent(field, 1)
                else:
                    sent(field, 0)
                advance(field, slot, 2 * pair + slot)
                if slot == 0:
                    send(field, 1)
                else:
                    @pl.when(pair < STEPS // 2 - 1)
                    def _():
                        send(field, 0)

    theirs = pl.ds((1 - sa) * half, half)
    own = pl.ds(sa * half, half)
    swap = pltpu.make_async_remote_copy(
        src_ref=corr.at[theirs], dst_ref=other, send_sem=sum_sem.at[0], recv_sem=sum_sem.at[1],
        device_id={"sa": 1 - sa}, device_id_type=MESH,
    )
    swap.start()
    stores = [
        pltpu.make_async_copy(src.at[inner], dst, store_sem.at[n])
        for n, (src, dst) in enumerate(((s0, s_first), (s1, s_second), (r0, r_first), (r1, r_second)))
    ]
    for store in stores:
        store.start()
    sent(0, 1)
    sent(1, 1)
    swap.wait()
    mine[...] = (corr[own] + other[...]) * (1.0 / STEPS)
    last = pltpu.make_async_copy(mine, image, store_sem.at[4])
    last.start()
    for store in stores:
        store.wait()
    last.wait()


def body(s_now, s_later, r_now, r_later, courant, wave, traces, s_in, s_cr, r_in, r_cr):
    ni, nc, nz = courant.shape
    half = ni // 2
    wide = (ni + 2 * REACH, nc + 2 * SIDE, nz)
    hbm = pl.BlockSpec(memory_space=pl.ANY)
    vmem = pl.BlockSpec(memory_space=pltpu.VMEM)
    smem = pl.BlockSpec(memory_space=pltpu.SMEM)
    tile = jax.ShapeDtypeStruct((ni, nc, nz), F32)
    outs = pl.pallas_call(
        kernel,
        out_shape=[tile] * 4 + [jax.ShapeDtypeStruct((half, nc, nz), F32)],
        in_specs=[hbm] * 5 + [vmem] * 2 + [smem] * 2 + [vmem] * 2,
        out_specs=[hbm] * 5,
        scratch_shapes=[pltpu.VMEM(wide, F32)] * 4
        + [
            pltpu.VMEM((ni, nc, nz), F32),
            pltpu.VMEM((ni, nc, nz), F32),
            pltpu.VMEM((half, nc, nz), F32),
            pltpu.VMEM((half, nc, nz), F32),
            pltpu.VMEM((ni * nc, nz), BF16),
            pltpu.VMEM((ni * nc, nz), BF16),
            pltpu.VMEM((2 * nz, nz), BF16),
            pltpu.VMEM((2, 2 * nz, nz), BF16),
            pltpu.VMEM((2, 2, 2, ni, REACH, nz), F32),
            pltpu.VMEM((2, 2, 2, ni, REACH, nz), F32),
            pltpu.SemaphoreType.DMA((5,)),
            pltpu.SemaphoreType.DMA((2, 2, 4)),
            pltpu.SemaphoreType.DMA((2, 2, 4)),
            pltpu.SemaphoreType.DMA((2,)),
            pltpu.SemaphoreType.DMA((5,)),
        ],
        compiler_params=pltpu.CompilerParams(
            collective_id=0, has_side_effects=True, vmem_limit_bytes=62 * 1024 * 1024
        ),
        name="window",
    )(s_now[0], s_later[0], r_now[0], r_later[0], courant, wave, traces, s_in, s_cr, r_in, r_cr)
    return tuple(out[None] for out in outs[:4]) + (outs[4],)


def solution(mesh):
    field = P(("groups", "sa"), "gx", "gy", None)
    in_specs = (
        (field,) * 4
        + (P("gx", "gy", None), P(("groups", "sa"), None), P(("groups", "sa"), None, None))
        + (P(("groups", "sa")),) * 2
        + (P(("groups", "sa"), None),) * 2
    )
    out_specs = (field,) * 4 + (P(("groups", "gx", "sa"), "gy", None),)
    return jax.shard_map(body, mesh=mesh, in_specs=in_specs, out_specs=out_specs, check_vma=False)
```

```python
import functools

import jax
import jax.numpy as jnp
from jax import lax
from jax.experimental import pallas as pl
from jax.experimental.pallas import tpu as pltpu
from jax.sharding import PartitionSpec as P

SRC_DEPTH = 3
REC_DEPTH = 2
STEPS = 12
REACH = 4
SIDE = 8
PLANES = 4

COEFFS = (-205.0 / 72.0, 8.0 / 5.0, -1.0 / 5.0, 8.0 / 315.0, -1.0 / 560.0)
MESH = pl.DeviceIdType.MESH
BF16 = jnp.bfloat16
F32 = jnp.float32


def halves(values):
    high = values.astype(BF16)
    low = (values - high.astype(F32)).astype(BF16)
    return high, low


def kernel(
    s_now, s_later, r_now, r_later, speed_in,
    wave, traces, s_in, s_cr, r_in, r_cr,
    s_first, s_second, r_first, r_second, image,
    s0, s1, r0, r1, speed, corr, other, mine, factors, weight, product, records,
    x_out, x_in, load_sem, send_sem, recv_sem, sum_sem, store_sem,
):
    ni, nc, nz = speed.shape
    cells = ni * nc
    half = ni // 2
    gx, gy, sa = lax.axis_index("gx"), lax.axis_index("gy"), lax.axis_index("sa")
    last_x, last_y = lax.axis_size("gx") - 1, lax.axis_size("gy") - 1
    below, above = gx > 0, gx < last_x
    left, right = gy > 0, gy < last_y
    fields = ((s0, s1), (r0, r1))
    rows = pl.ds(SIDE, nc)
    inner = (pl.ds(REACH, ni), rows)

    loads = [
        pltpu.make_async_copy(src, dst, load_sem.at[n])
        for n, (src, dst) in enumerate(
            (
                (s_now, s0.at[inner]),
                (r_now, r0.at[inner]),
                (s_later, s1.at[inner]),
                (r_later, r1.at[inner]),
                (speed_in, speed),
            )
        )
    ]
    for load in loads:
        load.start()

    ways = (
        ({"gx": gx - 1}, below, above),
        ({"gx": gx + 1}, above, below),
        ({"gy": gy - 1}, left, right),
        ({"gy": gy + 1}, right, left),
    )
    barrier = pltpu.get_barrier_semaphore()
    for target, sends, _ in ways:
        @pl.when(sends)
        def _():
            pl.semaphore_signal(barrier, inc=1, device_id=target, device_id_type=MESH)
    pl.semaphore_signal(barrier, inc=1, device_id={"sa": 1 - sa}, device_id_type=MESH)

    def exchange(field, slot, way):
        buf = fields[field][slot]
        if way == 0:
            src, dst = buf.at[pl.ds(REACH, REACH), rows], buf.at[pl.ds(REACH + ni, REACH), rows]
        elif way == 1:
            src, dst = buf.at[pl.ds(ni, REACH), rows], buf.at[pl.ds(0, REACH), rows]
        else:
            src, dst = x_out.at[field, slot, way - 2], x_in.at[field, slot, way - 2]
        return pltpu.make_async_remote_copy(
            src_ref=src, dst_ref=dst,
            send_sem=send_sem.at[field, slot, way], recv_sem=recv_sem.at[field, slot, way],
            device_id=ways[way][0], device_id_type=MESH,
        )

    def send(field, slot):
        buf = fields[field][slot]
        for way in (2, 3, 0, 1):
            @pl.when(ways[way][1])
            def _():
                if way == 2:
                    x_out[field, slot, 0] = buf[REACH:REACH + ni, SIDE:SIDE + REACH, :]
                if way == 3:
                    x_out[field, slot, 1] = buf[REACH:REACH + ni, SIDE + nc - REACH:SIDE + nc, :]
                exchange(field, slot, way).start()

    def sent(field, slot):
        for way in range(4):
            @pl.when(ways[way][1])
            def _():
                exchange(field, slot, way).wait_send()

    def receive(field, slot):
        buf = fields[field][slot]
        for way in (2, 3, 0, 1):
            @pl.when(ways[way][2])
            def _():
                exchange(field, slot, way).wait_recv()
                if way == 2:
                    buf[REACH:REACH + ni, SIDE + nc:SIDE + nc + REACH, :] = x_in[field, slot, 0]
                if way == 3:
                    buf[REACH:REACH + ni, SIDE - REACH:SIDE, :] = x_in[field, slot, 1]

    for pair in fields:
        for buf in pair:
            @pl.when(jnp.logical_not(below))
            def _():
                buf[0:REACH, SIDE:SIDE + nc, :] = jnp.zeros((REACH, nc, nz), F32)
            @pl.when(jnp.logical_not(above))
            def _():
                buf[REACH + ni:, SIDE:SIDE + nc, :] = jnp.zeros((REACH, nc, nz), F32)
            @pl.when(jnp.logical_not(left))
            def _():
                buf[REACH:REACH + ni, SIDE - REACH:SIDE, :] = jnp.zeros((ni, REACH, nz), F32)
            @pl.when(jnp.logical_not(right))
            def _():
                buf[REACH:REACH + ni, SIDE + nc:SIDE + nc + REACH, :] = jnp.zeros((ni, REACH, nz), F32)

    peers = 1
    for _, sends, _ in ways:
        peers = peers + sends.astype(jnp.int32)
    pl.semaphore_wait(barrier, peers)
    loads[0].wait()
    send(0, 0)
    loads[1].wait()
    send(1, 0)

    line = lax.broadcasted_iota(jnp.int32, (nz, nz), 0)
    lane = lax.broadcasted_iota(jnp.int32, (nz, nz), 1)
    apart = jnp.abs(line - lane)
    band = jnp.zeros((nz, nz), F32)
    for distance in range(1, 5):
        band = jnp.where(apart == distance, COEFFS[distance], band)
    band_high, band_low = halves(band)
    for field in range(2):
        weight[field, 0:nz, :] = band_high
        weight[field, nz:2 * nz, :] = band_high
        weight[field, 2 * nz:3 * nz, :] = band_low

    pick = (lax.broadcasted_iota(jnp.int32, (nz, STEPS), 0) % 32
            == lax.broadcasted_iota(jnp.int32, (nz, STEPS), 1)).astype(F32)
    dot = functools.partial(lax.dot_general, precision=lax.Precision.HIGHEST, preferred_element_type=F32)
    for t in range(STEPS):
        records[t:t + 1, :] = traces[t]
    by_lane = dot(pick, records[...], (((1,), (0,)), ((), ())))
    wave_lane = dot(jnp.broadcast_to(wave[...], (8, STEPS)), pick, (((1,), (1,)), ((), ())))[0:1]

    def local(inline, cross):
        a, b = inline - gx * ni, cross - gy * nc
        inside = (a >= 0) & (a < ni) & (b >= 0) & (b < nc)
        return jnp.where(inside, a * nc + b, -1)

    where_r = local(r_in[...], r_cr[...])
    where_s = local(s_in[0], s_cr[0])
    part = PLANES * nc

    def terms(total):
        group = lax.broadcasted_iota(jnp.int32, (part, nz), 1) // 32
        first = total.astype(BF16).astype(F32)
        rest = total - first
        second = rest.astype(BF16).astype(F32)
        third = rest - second
        return jnp.where(group == 0, first, jnp.where(group == 1, second, jnp.where(group == 2, third, 0.0))).astype(BF16)

    @pl.loop(0, cells // part)
    def _(n):
        start = pl.multiple_of(n * part, part)
        index = lax.broadcasted_iota(jnp.int32, (part, 1), 0) + start
        hot = (index == where_r).astype(F32)
        factors[1, pl.ds(start, part), 3 * nz:] = terms(dot(hot, by_lane, (((1,), (1,)), ((), ()))))
        factors[0, pl.ds(start, part), 3 * nz:] = terms(jnp.where(index == where_s, wave_lane, 0.0))

    corr[...] = jnp.zeros_like(corr)
    for load in loads[2:]:
        load.wait()

    def depth(field, slot, moment):
        cur, new = fields[field][slot], fields[field][1 - slot]
        level = (SRC_DEPTH, REC_DEPTH)[field]
        spot = (line < 96) & (line % 32 == moment) & (lane == level)
        weight[field, 3 * nz:, :] = spot.astype(F32).astype(BF16)
        for low in range(0, ni, PLANES):
            at, row = low + REACH, low * nc
            high_part, low_part = halves(cur[at:at + PLANES, SIDE:SIDE + nc, :].reshape(part, nz))
            factors[field, row:row + part, 0:nz] = high_part
            factors[field, row:row + part, nz:2 * nz] = low_part
            factors[field, row:row + part, 2 * nz:3 * nz] = high_part
        product[...] = jnp.dot(factors[field], weight[field], preferred_element_type=F32)
        for low in range(0, ni, PLANES):
            at, row = low + REACH, low * nc
            here = (slice(at, at + PLANES), slice(SIDE, SIDE + nc))
            centre = cur[here]
            total = product[row:row + part, :].reshape(PLANES, nc, nz) + (3.0 * COEFFS[0]) * centre
            new[here] = (2.0 * centre - new[here]) + speed[low:low + PLANES] * total

    def update(field, slot, low, count, col):
        cur, new = fields[field][slot], fields[field][1 - slot]
        at, side = low + REACH, SIDE + col
        window = cur[low:low + count + 2 * REACH, side:side + 8, :]
        total = None
        for k in range(1, 5):
            around = (
                window[REACH + k:REACH + k + count] + window[REACH - k:REACH - k + count]
            ) + (cur[at:at + count, side + k:side + k + 8, :] + cur[at:at + count, side - k:side - k + 8, :])
            total = COEFFS[k] * around if total is None else total + COEFFS[k] * around
        here = (slice(at, at + count), slice(side, side + 8))
        new[here] = new[here] + speed[low:low + count, col:col + 8, :] * total

    def column(field, slot, col):
        for low in range(REACH, ni - REACH, 8):
            update(field, slot, low, 8, col)

    def edges(field, slot):
        @pl.when(left)
        def _():
            column(field, slot, 0)
        @pl.when(right)
        def _():
            column(field, slot, nc - 8)
        for low in (0, ni - REACH):
            for col in range(0, nc, 8):
                update(field, slot, low, REACH, col)

    def middle(field, slot):
        @pl.when(jnp.logical_not(left))
        def _():
            column(field, slot, 0)
        @pl.when(jnp.logical_not(right))
        def _():
            column(field, slot, nc - 8)
        for col in range(8, nc - 8, 8):
            column(field, slot, col)

    def correlate(slot):
        for low in range(0, ni, PLANES):
            here = (slice(low + REACH, low + REACH + PLANES), slice(SIDE, SIDE + nc))
            corr[low:low + PLANES] += fields[0][slot][here] * fields[1][slot][here]

    depth(0, 0, 0)
    depth(1, 0, 0)

    @pl.loop(0, STEPS // 2)
    def _(pair):
        more = pair < STEPS // 2 - 1
        for slot in range(2):
            moment = 2 * pair + slot
            for field in range(2):
                receive(field, slot)
                edges(field, slot)
                if slot == 0:
                    send(field, 1)
                else:
                    @pl.when(more)
                    def _():
                        send(field, 0)
            for field in range(2):
                middle(field, slot)
                sent(field, slot)
                if slot == 0:
                    depth(field, 1, moment + 1)
                else:
                    @pl.when(more)
                    def _():
                        depth(field, 0, moment + 1)
            correlate(1 - slot)

    theirs = pl.ds((1 - sa) * half, half)
    own = pl.ds(sa * half, half)
    swap = pltpu.make_async_remote_copy(
        src_ref=corr.at[theirs], dst_ref=other, send_sem=sum_sem.at[0], recv_sem=sum_sem.at[1],
        device_id={"sa": 1 - sa}, device_id_type=MESH,
    )
    swap.start()
    stores = [
        pltpu.make_async_copy(src.at[inner], dst, store_sem.at[n])
        for n, (src, dst) in enumerate(((s0, s_first), (s1, s_second), (r0, r_first), (r1, r_second)))
    ]
    for store in stores:
        store.start()
    swap.wait()
    mine[...] = (corr[own] + other[...]) * (1.0 / STEPS)
    last = pltpu.make_async_copy(mine, image, store_sem.at[4])
    last.start()
    for store in stores:
        store.wait()
    last.wait()


def leave(*refs):
    copies = [pltpu.make_async_copy(refs[n], refs[5 + n], refs[10].at[n]) for n in range(5)]
    for copy in copies:
        copy.start()
    for copy in copies:
        copy.wait()


def body(s_now, s_later, r_now, r_later, courant, wave, traces, s_in, s_cr, r_in, r_cr):
    ni, nc, nz = courant.shape
    half = ni // 2
    wide = (ni + 2 * REACH, nc + 2 * SIDE, nz)
    hbm = pl.BlockSpec(memory_space=pltpu.HBM)
    vmem = pl.BlockSpec(memory_space=pltpu.VMEM)
    smem = pl.BlockSpec(memory_space=pltpu.SMEM)
    tile = jax.ShapeDtypeStruct((ni, nc, nz), F32)
    outs = pl.pallas_call(
        kernel,
        out_shape=[tile] * 4 + [jax.ShapeDtypeStruct((half, nc, nz), F32)],
        in_specs=[hbm] * 5 + [vmem] * 2 + [smem] * 2 + [vmem] * 2,
        out_specs=[pl.BlockSpec(memory_space=pl.ANY)] * 5,
        scratch_shapes=[pltpu.VMEM(wide, F32)] * 4
        + [
            pltpu.VMEM((ni, nc, nz), F32),
            pltpu.VMEM((ni, nc, nz), F32),
            pltpu.VMEM((half, nc, nz), F32),
            pltpu.VMEM((half, nc, nz), F32),
            pltpu.VMEM((2, ni * nc, 4 * nz), BF16),
            pltpu.VMEM((2, 4 * nz, nz), BF16),
            pltpu.VMEM((ni * nc, nz), F32),
            pltpu.VMEM((STEPS, traces.shape[2]), F32),
            pltpu.VMEM((2, 2, 2, ni, REACH, nz), F32),
            pltpu.VMEM((2, 2, 2, ni, REACH, nz), F32),
            pltpu.SemaphoreType.DMA((5,)),
            pltpu.SemaphoreType.DMA((2, 2, 4)),
            pltpu.SemaphoreType.DMA((2, 2, 4)),
            pltpu.SemaphoreType.DMA((2,)),
            pltpu.SemaphoreType.DMA((5,)),
        ],
        compiler_params=pltpu.CompilerParams(
            collective_id=0, has_side_effects=True, vmem_limit_bytes=32 * 1024 * 1024
        ),
        name="window",
    )(s_now[0], s_later[0], r_now[0], r_later[0], courant, wave, jnp.transpose(traces, (1, 0, 2)), s_in, s_cr, r_in, r_cr)
    outs = pl.pallas_call(
        leave,
        out_shape=[jax.ShapeDtypeStruct(out.shape, F32) for out in outs],
        in_specs=[pl.BlockSpec(memory_space=pl.ANY)] * 5,
        out_specs=[hbm] * 5,
        scratch_shapes=[pltpu.SemaphoreType.DMA((5,))],
        name="leave",
    )(*outs)
    return tuple(out[None] for out in outs[:4]) + (outs[4],)


def solution(mesh):
    field = P(("groups", "sa"), "gx", "gy", None)
    in_specs = (
        (field,) * 4
        + (P("gx", "gy", None), P(("groups", "sa"), None), P(("groups", "sa"), None, None))
        + (P(("groups", "sa")),) * 2
        + (P(("groups", "sa"), None),) * 2
    )
    out_specs = (field,) * 4 + (P(("groups", "gx", "sa"), "gy", None),)
    return jax.shard_map(body, mesh=mesh, in_specs=in_specs, out_specs=out_specs, check_vma=False)
```

```python
import functools

import jax
import jax.numpy as jnp
from jax import lax
from jax.experimental import pallas as pl
from jax.experimental.pallas import tpu as pltpu
from jax.sharding import PartitionSpec as P

SRC_DEPTH = 3
REC_DEPTH = 2
STEPS = 12
REACH = 4
SIDE = 8
PLANES = 4

COEFFS = (-205.0 / 72.0, 8.0 / 5.0, -1.0 / 5.0, 8.0 / 315.0, -1.0 / 560.0)
MESH = pl.DeviceIdType.MESH
BF16 = jnp.bfloat16
F32 = jnp.float32


def halves(values):
    high = values.astype(BF16)
    low = (values - high.astype(F32)).astype(BF16)
    return high, low


def kernel(
    s_now, s_later, r_now, r_later, speed_in,
    wave, traces, s_in, s_cr, r_in, r_cr,
    s_first, s_second, r_first, r_second, image,
    s0, s1, r0, r1, speed, corr, other, mine, factors, weight, product, records,
    x_out, x_in, load_sem, send_sem, recv_sem, sum_sem, store_sem,
):
    ni, nc, nz = speed.shape
    cells = ni * nc
    half = ni // 2
    gx, gy, sa = lax.axis_index("gx"), lax.axis_index("gy"), lax.axis_index("sa")
    last_x, last_y = lax.axis_size("gx") - 1, lax.axis_size("gy") - 1
    below, above = gx > 0, gx < last_x
    left, right = gy > 0, gy < last_y
    fields = ((s0, s1), (r0, r1))
    rows = pl.ds(SIDE, nc)
    inner = (pl.ds(REACH, ni), rows)

    loads = [
        pltpu.make_async_copy(src, dst, load_sem.at[n])
        for n, (src, dst) in enumerate(
            (
                (s_now, s0.at[inner]),
                (r_now, r0.at[inner]),
                (s_later, s1.at[inner]),
                (r_later, r1.at[inner]),
                (speed_in, speed),
            )
        )
    ]
    for load in loads:
        load.start()

    ways = (
        ({"gx": gx - 1}, below, above),
        ({"gx": gx + 1}, above, below),
        ({"gy": gy - 1}, left, right),
        ({"gy": gy + 1}, right, left),
    )
    barrier = pltpu.get_barrier_semaphore()
    for target, sends, _ in ways:
        @pl.when(sends)
        def _():
            pl.semaphore_signal(barrier, inc=1, device_id=target, device_id_type=MESH)
    pl.semaphore_signal(barrier, inc=1, device_id={"sa": 1 - sa}, device_id_type=MESH)

    def exchange(field, slot, way):
        buf = fields[field][slot]
        if way == 0:
            src, dst = buf.at[pl.ds(REACH, REACH), rows], buf.at[pl.ds(REACH + ni, REACH), rows]
        elif way == 1:
            src, dst = buf.at[pl.ds(ni, REACH), rows], buf.at[pl.ds(0, REACH), rows]
        else:
            src, dst = x_out.at[field, slot, way - 2], x_in.at[field, slot, way - 2]
        return pltpu.make_async_remote_copy(
            src_ref=src, dst_ref=dst,
            send_sem=send_sem.at[field, slot, way], recv_sem=recv_sem.at[field, slot, way],
            device_id=ways[way][0], device_id_type=MESH,
        )

    def send(field, slot):
        buf = fields[field][slot]
        for way in (2, 3, 0, 1):
            @pl.when(ways[way][1])
            def _():
                if way == 2:
                    x_out[field, slot, 0] = buf[REACH:REACH + ni, SIDE:SIDE + REACH, :]
                if way == 3:
                    x_out[field, slot, 1] = buf[REACH:REACH + ni, SIDE + nc - REACH:SIDE + nc, :]
                exchange(field, slot, way).start()

    def sent(field, slot):
        for way in range(4):
            @pl.when(ways[way][1])
            def _():
                exchange(field, slot, way).wait_send()

    def receive(field, slot):
        buf = fields[field][slot]
        for way in (2, 3, 0, 1):
            @pl.when(ways[way][2])
            def _():
                exchange(field, slot, way).wait_recv()
                if way == 2:
                    buf[REACH:REACH + ni, SIDE + nc:SIDE + nc + REACH, :] = x_in[field, slot, 0]
                if way == 3:
                    buf[REACH:REACH + ni, SIDE - REACH:SIDE, :] = x_in[field, slot, 1]

    for pair in fields:
        for buf in pair:
            @pl.when(jnp.logical_not(below))
            def _():
                buf[0:REACH, SIDE:SIDE + nc, :] = jnp.zeros((REACH, nc, nz), F32)
            @pl.when(jnp.logical_not(above))
            def _():
                buf[REACH + ni:, SIDE:SIDE + nc, :] = jnp.zeros((REACH, nc, nz), F32)
            @pl.when(jnp.logical_not(left))
            def _():
                buf[REACH:REACH + ni, SIDE - REACH:SIDE, :] = jnp.zeros((ni, REACH, nz), F32)
            @pl.when(jnp.logical_not(right))
            def _():
                buf[REACH:REACH + ni, SIDE + nc:SIDE + nc + REACH, :] = jnp.zeros((ni, REACH, nz), F32)

    peers = 1
    for _, sends, _ in ways:
        peers = peers + sends.astype(jnp.int32)
    pl.semaphore_wait(barrier, peers)
    loads[0].wait()
    send(0, 0)
    loads[1].wait()
    send(1, 0)

    line = lax.broadcasted_iota(jnp.int32, (nz, nz), 0)
    lane = lax.broadcasted_iota(jnp.int32, (nz, nz), 1)
    apart = jnp.abs(line - lane)
    band = jnp.zeros((nz, nz), F32)
    for distance in range(1, 5):
        band = jnp.where(apart == distance, COEFFS[distance], band)
    band_high, band_low = halves(band)
    for field in range(2):
        weight[field, 0:nz, :] = band_high
        weight[field, nz:2 * nz, :] = band_high
        weight[field, 2 * nz:3 * nz, :] = band_low

    pick = (lax.broadcasted_iota(jnp.int32, (nz, STEPS), 0) % 32
            == lax.broadcasted_iota(jnp.int32, (nz, STEPS), 1)).astype(F32)
    dot = functools.partial(lax.dot_general, precision=lax.Precision.HIGHEST, preferred_element_type=F32)
    for t in range(STEPS):
        records[t:t + 1, :] = traces[t]
    by_lane = dot(pick, records[...], (((1,), (0,)), ((), ())))
    wave_lane = dot(jnp.broadcast_to(wave[...], (8, STEPS)), pick, (((1,), (1,)), ((), ())))[0:1]

    def local(inline, cross):
        a, b = inline - gx * ni, cross - gy * nc
        inside = (a >= 0) & (a < ni) & (b >= 0) & (b < nc)
        return jnp.where(inside, a * nc + b, -1)

    where_r = local(r_in[...], r_cr[...])
    where_s = local(s_in[0], s_cr[0])
    part = PLANES * nc

    def terms(total):
        group = lax.broadcasted_iota(jnp.int32, (part, nz), 1) // 32
        first = total.astype(BF16).astype(F32)
        rest = total - first
        second = rest.astype(BF16).astype(F32)
        third = rest - second
        return jnp.where(group == 0, first, jnp.where(group == 1, second, jnp.where(group == 2, third, 0.0))).astype(BF16)

    @pl.loop(0, cells // part)
    def _(n):
        start = pl.multiple_of(n * part, part)
        index = lax.broadcasted_iota(jnp.int32, (part, 1), 0) + start
        hot = (index == where_r).astype(F32)
        factors[1, pl.ds(start, part), 3 * nz:] = terms(dot(hot, by_lane, (((1,), (1,)), ((), ()))))
        factors[0, pl.ds(start, part), 3 * nz:] = terms(jnp.where(index == where_s, wave_lane, 0.0))

    corr[...] = jnp.zeros_like(corr)
    for load in loads[2:]:
        load.wait()

    def depth(field, slot, moment):
        cur, new = fields[field][slot], fields[field][1 - slot]
        level = (SRC_DEPTH, REC_DEPTH)[field]
        spot = (line < 96) & (line % 32 == moment) & (lane == level)
        weight[field, 3 * nz:, :] = spot.astype(F32).astype(BF16)
        for low in range(0, ni, PLANES):
            at, row = low + REACH, low * nc
            high_part, low_part = halves(cur[at:at + PLANES, SIDE:SIDE + nc, :].reshape(part, nz))
            factors[field, row:row + part, 0:nz] = high_part
            factors[field, row:row + part, nz:2 * nz] = low_part
            factors[field, row:row + part, 2 * nz:3 * nz] = high_part
        product[...] = jnp.dot(factors[field], weight[field], preferred_element_type=F32)
        for low in range(0, ni, PLANES):
            at, row = low + REACH, low * nc
            here = (slice(at, at + PLANES), slice(SIDE, SIDE + nc))
            centre = cur[here]
            total = product[row:row + part, :].reshape(PLANES, nc, nz) + (3.0 * COEFFS[0]) * centre
            new[here] = (2.0 * centre - new[here]) + speed[low:low + PLANES] * total

    def update(field, slot, low, count, col):
        cur, new = fields[field][slot], fields[field][1 - slot]
        at, side = low + REACH, SIDE + col
        window = cur[low:low + count + 2 * REACH, side:side + 8, :]
        total = None
        for k in range(1, 5):
            around = (
                window[REACH + k:REACH + k + count] + window[REACH - k:REACH - k + count]
            ) + (cur[at:at + count, side + k:side + k + 8, :] + cur[at:at + count, side - k:side - k + 8, :])
            total = COEFFS[k] * around if total is None else total + COEFFS[k] * around
        here = (slice(at, at + count), slice(side, side + 8))
        new[here] = new[here] + speed[low:low + count, col:col + 8, :] * total

    def column(field, slot, col):
        for low in range(REACH, ni - REACH, 8):
            update(field, slot, low, 8, col)

    def edges(field, slot):
        @pl.when(left)
        def _():
            column(field, slot, 0)
        @pl.when(right)
        def _():
            column(field, slot, nc - 8)
        for low in (0, ni - REACH):
            for col in range(0, nc, 8):
                update(field, slot, low, REACH, col)

    def middle(field, slot):
        @pl.when(jnp.logical_not(left))
        def _():
            column(field, slot, 0)
        @pl.when(jnp.logical_not(right))
        def _():
            column(field, slot, nc - 8)
        for col in range(8, nc - 8, 8):
            column(field, slot, col)

    def correlate(slot):
        for low in range(0, ni, PLANES):
            here = (slice(low + REACH, low + REACH + PLANES), slice(SIDE, SIDE + nc))
            corr[low:low + PLANES] += fields[0][slot][here] * fields[1][slot][here]

    depth(0, 0, 0)
    depth(1, 0, 0)

    @pl.loop(0, STEPS // 2)
    def _(pair):
        more = pair < STEPS // 2 - 1
        for slot in range(2):
            moment = 2 * pair + slot
            for field in range(2):
                receive(field, slot)
                edges(field, slot)
                if slot == 0:
                    send(field, 1)
                else:
                    @pl.when(more)
                    def _():
                        send(field, 0)
            for field in range(2):
                middle(field, slot)
                sent(field, slot)
                if slot == 0:
                    depth(field, 1, moment + 1)
                else:
                    @pl.when(more)
                    def _():
                        depth(field, 0, moment + 1)
            correlate(1 - slot)

    theirs = pl.ds((1 - sa) * half, half)
    own = pl.ds(sa * half, half)
    swap = pltpu.make_async_remote_copy(
        src_ref=corr.at[theirs], dst_ref=other, send_sem=sum_sem.at[0], recv_sem=sum_sem.at[1],
        device_id={"sa": 1 - sa}, device_id_type=MESH,
    )
    swap.start()
    stores = [
        pltpu.make_async_copy(src.at[inner], dst, store_sem.at[n])
        for n, (src, dst) in enumerate(((s0, s_first), (s1, s_second), (r0, r_first), (r1, r_second)))
    ]
    for store in stores:
        store.start()
    swap.wait()
    mine[...] = (corr[own] + other[...]) * (1.0 / STEPS)
    last = pltpu.make_async_copy(mine, image, store_sem.at[4])
    last.start()
    for store in stores:
        store.wait()
    last.wait()


def leave(*refs):
    sems = refs[15]
    loads = [pltpu.make_async_copy(refs[n], refs[10 + n], sems.at[0, n]) for n in range(5)]
    stores = [pltpu.make_async_copy(refs[10 + n], refs[5 + n], sems.at[1, n]) for n in range(5)]
    for load in loads:
        load.start()
    for load, store in zip(loads, stores):
        load.wait()
        store.start()
    for store in stores:
        store.wait()


def body(s_now, s_later, r_now, r_later, courant, wave, traces, s_in, s_cr, r_in, r_cr):
    ni, nc, nz = courant.shape
    half = ni // 2
    wide = (ni + 2 * REACH, nc + 2 * SIDE, nz)
    hbm = pl.BlockSpec(memory_space=pltpu.HBM)
    vmem = pl.BlockSpec(memory_space=pltpu.VMEM)
    smem = pl.BlockSpec(memory_space=pltpu.SMEM)
    tile = jax.ShapeDtypeStruct((ni, nc, nz), F32)
    outs = pl.pallas_call(
        kernel,
        out_shape=[tile] * 4 + [jax.ShapeDtypeStruct((half, nc, nz), F32)],
        in_specs=[hbm] * 5 + [vmem] * 2 + [smem] * 2 + [vmem] * 2,
        out_specs=[pl.BlockSpec(memory_space=pl.ANY)] * 5,
        scratch_shapes=[pltpu.VMEM(wide, F32)] * 4
        + [
            pltpu.VMEM((ni, nc, nz), F32),
            pltpu.VMEM((ni, nc, nz), F32),
            pltpu.VMEM((half, nc, nz), F32),
            pltpu.VMEM((half, nc, nz), F32),
            pltpu.VMEM((2, ni * nc, 4 * nz), BF16),
            pltpu.VMEM((2, 4 * nz, nz), BF16),
            pltpu.VMEM((ni * nc, nz), F32),
            pltpu.VMEM((STEPS, traces.shape[2]), F32),
            pltpu.VMEM((2, 2, 2, ni, REACH, nz), F32),
            pltpu.VMEM((2, 2, 2, ni, REACH, nz), F32),
            pltpu.SemaphoreType.DMA((5,)),
            pltpu.SemaphoreType.DMA((2, 2, 4)),
            pltpu.SemaphoreType.DMA((2, 2, 4)),
            pltpu.SemaphoreType.DMA((2,)),
            pltpu.SemaphoreType.DMA((5,)),
        ],
        compiler_params=pltpu.CompilerParams(
            collective_id=0, has_side_effects=True, vmem_limit_bytes=62 * 1024 * 1024
        ),
        name="window",
    )(s_now[0], s_later[0], r_now[0], r_later[0], courant, wave, jnp.transpose(traces, (1, 0, 2)), s_in, s_cr, r_in, r_cr)
    outs = pl.pallas_call(
        leave,
        out_shape=[jax.ShapeDtypeStruct(out.shape, F32) for out in outs],
        in_specs=[pl.BlockSpec(memory_space=pl.ANY)] * 5,
        out_specs=[hbm] * 5,
        scratch_shapes=[pltpu.VMEM(out.shape, F32) for out in outs] + [pltpu.SemaphoreType.DMA((2, 5))],
        compiler_params=pltpu.CompilerParams(vmem_limit_bytes=62 * 1024 * 1024),
        name="leave",
    )(*outs)
    return tuple(out[None] for out in outs[:4]) + (outs[4],)


def solution(mesh):
    field = P(("groups", "sa"), "gx", "gy", None)
    in_specs = (
        (field,) * 4
        + (P("gx", "gy", None), P(("groups", "sa"), None), P(("groups", "sa"), None, None))
        + (P(("groups", "sa")),) * 2
        + (P(("groups", "sa"), None),) * 2
    )
    out_specs = (field,) * 4 + (P(("groups", "gx", "sa"), "gy", None),)
    return jax.shard_map(body, mesh=mesh, in_specs=in_specs, out_specs=out_specs, check_vma=False)
```

```python
import functools

import jax
import jax.numpy as jnp
from jax import lax
from jax.experimental import pallas as pl
from jax.experimental.pallas import tpu as pltpu
from jax.sharding import PartitionSpec as P

SRC_DEPTH = 3
REC_DEPTH = 2
STEPS = 12
REACH = 4
SIDE = 8
PLANES = 4

COEFFS = (-205.0 / 72.0, 8.0 / 5.0, -1.0 / 5.0, 8.0 / 315.0, -1.0 / 560.0)
MESH = pl.DeviceIdType.MESH
BF16 = jnp.bfloat16
F32 = jnp.float32


def halves(values):
    high = values.astype(BF16)
    low = (values - high.astype(F32)).astype(BF16)
    return high, low


def kernel(
    s_now, s_later, r_now, r_later, speed_in,
    wave, traces, s_in, s_cr, r_in, r_cr,
    s_first, s_second, r_first, r_second, image,
    s0, s1, r0, r1, speed, corr, other, mine, factors, weight, product, cross_table, records,
    x_out, x_in, load_sem, send_sem, recv_sem, sum_sem, store_sem,
):
    ni, nc, nz = speed.shape
    cells = ni * nc
    half = ni // 2
    gx, gy, sa = lax.axis_index("gx"), lax.axis_index("gy"), lax.axis_index("sa")
    last_x, last_y = lax.axis_size("gx") - 1, lax.axis_size("gy") - 1
    below, above = gx > 0, gx < last_x
    left, right = gy > 0, gy < last_y
    fields = ((s0, s1), (r0, r1))
    rows = pl.ds(SIDE, nc)
    inner = (pl.ds(REACH, ni), rows)

    loads = [
        pltpu.make_async_copy(src, dst, load_sem.at[n])
        for n, (src, dst) in enumerate(
            (
                (s_now, s0.at[inner]),
                (r_now, r0.at[inner]),
                (s_later, s1.at[inner]),
                (r_later, r1.at[inner]),
                (speed_in, speed),
            )
        )
    ]
    for load in loads:
        load.start()

    ways = (
        ({"gx": gx - 1}, below, above),
        ({"gx": gx + 1}, above, below),
        ({"gy": gy - 1}, left, right),
        ({"gy": gy + 1}, right, left),
    )
    barrier = pltpu.get_barrier_semaphore()
    for target, sends, _ in ways:
        @pl.when(sends)
        def _():
            pl.semaphore_signal(barrier, inc=1, device_id=target, device_id_type=MESH)
    pl.semaphore_signal(barrier, inc=1, device_id={"sa": 1 - sa}, device_id_type=MESH)

    def exchange(field, slot, way):
        buf = fields[field][slot]
        if way == 0:
            src, dst = buf.at[pl.ds(REACH, REACH), rows], buf.at[pl.ds(REACH + ni, REACH), rows]
        elif way == 1:
            src, dst = buf.at[pl.ds(ni, REACH), rows], buf.at[pl.ds(0, REACH), rows]
        else:
            src, dst = x_out.at[field, slot, way - 2], x_in.at[field, slot, way - 2]
        return pltpu.make_async_remote_copy(
            src_ref=src, dst_ref=dst,
            send_sem=send_sem.at[field, slot, way], recv_sem=recv_sem.at[field, slot, way],
            device_id=ways[way][0], device_id_type=MESH,
        )

    def send(field, slot):
        buf = fields[field][slot]
        for way in (2, 3, 0, 1):
            @pl.when(ways[way][1])
            def _():
                if way == 2:
                    x_out[field, slot, 0] = buf[REACH:REACH + ni, SIDE:SIDE + REACH, :]
                if way == 3:
                    x_out[field, slot, 1] = buf[REACH:REACH + ni, SIDE + nc - REACH:SIDE + nc, :]
                exchange(field, slot, way).start()

    def sent(field, slot):
        for way in range(4):
            @pl.when(ways[way][1])
            def _():
                exchange(field, slot, way).wait_send()

    def receive(field, slot):
        buf = fields[field][slot]
        for way in (2, 3, 0, 1):
            @pl.when(ways[way][2])
            def _():
                exchange(field, slot, way).wait_recv()
                if way == 2:
                    buf[REACH:REACH + ni, SIDE + nc:SIDE + nc + REACH, :] = x_in[field, slot, 0]
                if way == 3:
                    buf[REACH:REACH + ni, SIDE - REACH:SIDE, :] = x_in[field, slot, 1]

    for pair in fields:
        for buf in pair:
            @pl.when(jnp.logical_not(below))
            def _():
                buf[0:REACH, SIDE:SIDE + nc, :] = jnp.zeros((REACH, nc, nz), F32)
            @pl.when(jnp.logical_not(above))
            def _():
                buf[REACH + ni:, SIDE:SIDE + nc, :] = jnp.zeros((REACH, nc, nz), F32)
            @pl.when(jnp.logical_not(left))
            def _():
                buf[REACH:REACH + ni, SIDE - REACH:SIDE, :] = jnp.zeros((ni, REACH, nz), F32)
            @pl.when(jnp.logical_not(right))
            def _():
                buf[REACH:REACH + ni, SIDE + nc:SIDE + nc + REACH, :] = jnp.zeros((ni, REACH, nz), F32)

    peers = 1
    for _, sends, _ in ways:
        peers = peers + sends.astype(jnp.int32)
    pl.semaphore_wait(barrier, peers)
    loads[0].wait()
    send(0, 0)
    loads[1].wait()
    send(1, 0)

    line = lax.broadcasted_iota(jnp.int32, (nz, nz), 0)
    lane = lax.broadcasted_iota(jnp.int32, (nz, nz), 1)
    apart = jnp.abs(line - lane)
    band = jnp.zeros((nz, nz), F32)
    for distance in range(1, 5):
        band = jnp.where(apart == distance, COEFFS[distance], band)
    band_high, band_low = halves(band)
    for field in range(2):
        weight[field, 0:nz, :] = band_high
        weight[field, nz:2 * nz, :] = band_high
        weight[field, 2 * nz:3 * nz, :] = band_low

    pick = (lax.broadcasted_iota(jnp.int32, (nz, STEPS), 0) % 32
            == lax.broadcasted_iota(jnp.int32, (nz, STEPS), 1)).astype(F32)
    dot = functools.partial(lax.dot_general, precision=lax.Precision.HIGHEST, preferred_element_type=F32)
    for t in range(STEPS):
        records[t:t + 1, :] = traces[t]
    by_lane = dot(pick, records[...], (((1,), (0,)), ((), ())))
    wave_lane = dot(jnp.broadcast_to(wave[...], (8, STEPS)), pick, (((1,), (1,)), ((), ())))[0:1]

    def local(inline, cross):
        a, b = inline - gx * ni, cross - gy * nc
        inside = (a >= 0) & (a < ni) & (b >= 0) & (b < nc)
        return jnp.where(inside, a * nc + b, -1)

    where_r = local(r_in[...], r_cr[...])
    where_s = local(s_in[0], s_cr[0])
    part = PLANES * nc

    def terms(total):
        group = lax.broadcasted_iota(jnp.int32, (part, nz), 1) // 32
        first = total.astype(BF16).astype(F32)
        rest = total - first
        second = rest.astype(BF16).astype(F32)
        third = rest - second
        return jnp.where(group == 0, first, jnp.where(group == 1, second, jnp.where(group == 2, third, 0.0))).astype(BF16)

    @pl.loop(0, cells // part)
    def _(n):
        start = pl.multiple_of(n * part, part)
        index = lax.broadcasted_iota(jnp.int32, (part, 1), 0) + start
        hot = (index == where_r).astype(F32)
        factors[1, pl.ds(start, part), 3 * nz:] = terms(dot(hot, by_lane, (((1,), (1,)), ((), ()))))
        factors[0, pl.ds(start, part), 3 * nz:] = terms(jnp.where(index == where_s, wave_lane, 0.0))

    corr[...] = jnp.zeros_like(corr)
    for load in loads[2:]:
        load.wait()

    spare = -3 * nc % 16
    to = lax.broadcasted_iota(jnp.int32, (nc, 3 * nc + spare), 0)
    of = lax.broadcasted_iota(jnp.int32, (nc, 3 * nc + spare), 1)
    cross = jnp.zeros((nc, 3 * nc + spare), F32)
    for distance in range(1, 5):
        cross = jnp.where(jnp.abs(to - of % nc) == distance, COEFFS[distance], cross)
    cross_high = cross.astype(BF16).astype(F32)
    group = of // nc
    cross_table[...] = jnp.where(
        group < 2, cross_high, jnp.where(group == 2, cross - cross_high, 0.0)
    ).astype(BF16)
    fill = [jnp.zeros((spare, nz), F32)] if spare else []

    def depth(field, slot, moment):
        cur, new = fields[field][slot], fields[field][1 - slot]
        level = (SRC_DEPTH, REC_DEPTH)[field]
        spot = (line < 96) & (line % 32 == moment) & (lane == level)
        weight[field, 3 * nz:, :] = spot.astype(F32).astype(BF16)
        for low in range(0, ni, PLANES):
            at, row = low + REACH, low * nc
            high_part, low_part = halves(cur[at:at + PLANES, SIDE:SIDE + nc, :].reshape(part, nz))
            factors[field, row:row + part, 0:nz] = high_part
            factors[field, row:row + part, nz:2 * nz] = low_part
            factors[field, row:row + part, 2 * nz:3 * nz] = high_part
        cross_band = cross_table[...]
        product[...] = jnp.dot(factors[field], weight[field], preferred_element_type=F32)
        for low in range(0, ni, PLANES):
            at, row = low + REACH, low * nc
            here = (slice(at, at + PLANES), slice(SIDE, SIDE + nc))
            centre = cur[here]
            first = centre.astype(BF16).astype(F32)
            rest = centre - first
            across = []
            for p in range(0, PLANES, 2):
                stacks = [
                    jnp.concatenate([first[p + n], rest[p + n], first[p + n]] + fill, axis=0)
                    for n in range(2)
                ]
                both = jnp.dot(
                    cross_band, jnp.concatenate(stacks, axis=1).astype(BF16), preferred_element_type=F32
                )
                across += [both[:, :nz], both[:, nz:]]
            total = product[row:row + part, :].reshape(PLANES, nc, nz) + (3.0 * COEFFS[0]) * centre
            total = total + jnp.stack(across)
            new[here] = (2.0 * centre - new[here]) + speed[low:low + PLANES] * total

    def update(field, slot, low, count, col):
        cur, new = fields[field][slot], fields[field][1 - slot]
        at, side = low + REACH, SIDE + col
        window = cur[low:low + count + 2 * REACH, side:side + 8, :]
        row = lax.broadcasted_iota(jnp.int32, (count, 8, nz), 1)
        total = None
        for k in range(1, 5):
            around = window[REACH + k:REACH + k + count] + window[REACH - k:REACH - k + count]
            if col == 0:
                around = around + jnp.where(row < k, cur[at:at + count, side - k:side - k + 8, :], 0.0)
            if col == nc - 8:
                around = around + jnp.where(row >= 8 - k, cur[at:at + count, side + k:side + k + 8, :], 0.0)
            total = COEFFS[k] * around if total is None else total + COEFFS[k] * around
        here = (slice(at, at + count), slice(side, side + 8))
        new[here] = new[here] + speed[low:low + count, col:col + 8, :] * total

    def column(field, slot, col):
        for low in range(REACH, ni - REACH, 8):
            update(field, slot, low, 8, col)

    def edges(field, slot):
        @pl.when(left)
        def _():
            column(field, slot, 0)
        @pl.when(right)
        def _():
            column(field, slot, nc - 8)
        for low in (0, ni - REACH):
            for col in range(0, nc, 8):
                update(field, slot, low, REACH, col)

    def middle(field, slot):
        @pl.when(jnp.logical_not(left))
        def _():
            column(field, slot, 0)
        @pl.when(jnp.logical_not(right))
        def _():
            column(field, slot, nc - 8)
        for col in range(8, nc - 8, 8):
            column(field, slot, col)

    def correlate(slot):
        for low in range(0, ni, PLANES):
            here = (slice(low + REACH, low + REACH + PLANES), slice(SIDE, SIDE + nc))
            corr[low:low + PLANES] += fields[0][slot][here] * fields[1][slot][here]

    depth(0, 0, 0)
    depth(1, 0, 0)

    @pl.loop(0, STEPS // 2)
    def _(pair):
        more = pair < STEPS // 2 - 1
        for slot in range(2):
            moment = 2 * pair + slot
            for field in range(2):
                receive(field, slot)
                edges(field, slot)
                if slot == 0:
                    send(field, 1)
                else:
                    @pl.when(more)
                    def _():
                        send(field, 0)
            for field in range(2):
                middle(field, slot)
                sent(field, slot)
                if slot == 0:
                    depth(field, 1, moment + 1)
                else:
                    @pl.when(more)
                    def _():
                        depth(field, 0, moment + 1)
            correlate(1 - slot)

    theirs = pl.ds((1 - sa) * half, half)
    own = pl.ds(sa * half, half)
    swap = pltpu.make_async_remote_copy(
        src_ref=corr.at[theirs], dst_ref=other, send_sem=sum_sem.at[0], recv_sem=sum_sem.at[1],
        device_id={"sa": 1 - sa}, device_id_type=MESH,
    )
    swap.start()
    stores = [
        pltpu.make_async_copy(src.at[inner], dst, store_sem.at[n])
        for n, (src, dst) in enumerate(((s0, s_first), (s1, s_second), (r0, r_first), (r1, r_second)))
    ]
    for store in stores:
        store.start()
    swap.wait()
    mine[...] = (corr[own] + other[...]) * (1.0 / STEPS)
    last = pltpu.make_async_copy(mine, image, store_sem.at[4])
    last.start()
    for store in stores:
        store.wait()
    last.wait()


def leave(*refs):
    sems = refs[15]
    loads = [pltpu.make_async_copy(refs[n], refs[10 + n], sems.at[0, n]) for n in range(5)]
    stores = [pltpu.make_async_copy(refs[10 + n], refs[5 + n], sems.at[1, n]) for n in range(5)]
    for load in loads:
        load.start()
    for load, store in zip(loads, stores):
        load.wait()
        store.start()
    for store in stores:
        store.wait()


def body(s_now, s_later, r_now, r_later, courant, wave, traces, s_in, s_cr, r_in, r_cr):
    ni, nc, nz = courant.shape
    half = ni // 2
    wide = (ni + 2 * REACH, nc + 2 * SIDE, nz)
    hbm = pl.BlockSpec(memory_space=pltpu.HBM)
    vmem = pl.BlockSpec(memory_space=pltpu.VMEM)
    smem = pl.BlockSpec(memory_space=pltpu.SMEM)
    tile = jax.ShapeDtypeStruct((ni, nc, nz), F32)
    outs = pl.pallas_call(
        kernel,
        out_shape=[tile] * 4 + [jax.ShapeDtypeStruct((half, nc, nz), F32)],
        in_specs=[hbm] * 5 + [vmem] * 2 + [smem] * 2 + [vmem] * 2,
        out_specs=[pl.BlockSpec(memory_space=pl.ANY)] * 5,
        scratch_shapes=[pltpu.VMEM(wide, F32)] * 4
        + [
            pltpu.VMEM((ni, nc, nz), F32),
            pltpu.VMEM((ni, nc, nz), F32),
            pltpu.VMEM((half, nc, nz), F32),
            pltpu.VMEM((half, nc, nz), F32),
            pltpu.VMEM((2, ni * nc, 4 * nz), BF16),
            pltpu.VMEM((2, 4 * nz, nz), BF16),
            pltpu.VMEM((ni * nc, nz), F32),
            pltpu.VMEM((nc, 3 * nc + -3 * nc % 16), BF16),
            pltpu.VMEM((STEPS, traces.shape[2]), F32),
            pltpu.VMEM((2, 2, 2, ni, REACH, nz), F32),
            pltpu.VMEM((2, 2, 2, ni, REACH, nz), F32),
            pltpu.SemaphoreType.DMA((5,)),
            pltpu.SemaphoreType.DMA((2, 2, 4)),
            pltpu.SemaphoreType.DMA((2, 2, 4)),
            pltpu.SemaphoreType.DMA((2,)),
            pltpu.SemaphoreType.DMA((5,)),
        ],
        compiler_params=pltpu.CompilerParams(
            collective_id=0, has_side_effects=True, vmem_limit_bytes=62 * 1024 * 1024
        ),
        name="window",
    )(s_now[0], s_later[0], r_now[0], r_later[0], courant, wave, jnp.transpose(traces, (1, 0, 2)), s_in, s_cr, r_in, r_cr)
    outs = pl.pallas_call(
        leave,
        out_shape=[jax.ShapeDtypeStruct(out.shape, F32) for out in outs],
        in_specs=[pl.BlockSpec(memory_space=pl.ANY)] * 5,
        out_specs=[hbm] * 5,
        scratch_shapes=[pltpu.VMEM(out.shape, F32) for out in outs] + [pltpu.SemaphoreType.DMA((2, 5))],
        compiler_params=pltpu.CompilerParams(vmem_limit_bytes=62 * 1024 * 1024),
        name="leave",
    )(*outs)
    return tuple(out[None] for out in outs[:4]) + (outs[4],)


def solution(mesh):
    field = P(("groups", "sa"), "gx", "gy", None)
    in_specs = (
        (field,) * 4
        + (P("gx", "gy", None), P(("groups", "sa"), None), P(("groups", "sa"), None, None))
        + (P(("groups", "sa")),) * 2
        + (P(("groups", "sa"), None),) * 2
    )
    out_specs = (field,) * 4 + (P(("groups", "gx", "sa"), "gy", None),)
    return jax.shard_map(body, mesh=mesh, in_specs=in_specs, out_specs=out_specs, check_vma=False)
```
